32 devices in a mesh: grp: 2 (over x), chan: 4 (over y, core), ctx: 4 (over z).
Axes of the slice: x: 2, y: 2, z: 4, core: 2. Of those that a mesh axis runs over, the one named last changes fastest.
Arguments:
- features: bfloat16 [4096, 4096], P(('grp', 'ctx'), 'chan'), parts along dimension 0, may hold values from -6 to 6
- filter_taps: bfloat16 [2048, 4096], P(None, 'chan'), may hold values from -0.125 to 0.125
- skip_gain: float32 [4096], P('chan'), may hold values from -4 to 4
- in_weight: bfloat16 [4096, 3, 4096], P(None, None, 'chan'), may hold values from -0.09375 to 0.09375
- out_weight: bfloat16 [4096, 4096], P(None, 'chan'), may hold values from -0.125 to 0.125
Outputs:
- layer_out: bfloat16 [4096, 4096], P(('grp', 'ctx'), 'chan'), parts along dimension 0
The draws below stay inside these ranges and needn't reach their ends.
There are 2 independent parts, one for each index of `grp`. The reference program is written for one: setup_inputs(seed, part) draws one part's arguments, and reference() takes and returns one part's arrays. A program takes and returns all parts, laid end to end along the dimension named above; an argument that names none is the same for every part. Nothing has to cross between parts.
All inputs are finite; a program needn't handle non-finite values.
Results may differ from the reference program's by a relative error of at most 0.013.
Values may be sent and summed in bfloat16 or wider, within the bound.
A program may use at most 320 MiB of HBM per device.

```python
import math
import jax
import jax.numpy as jnp
from jax import lax

D = 4096
P_SIZE = 128
LENGTH = 2048


def spiked(values, rng, source, target, parts, factor):
    owner, partner = [(jnp.arange(values.shape[position]) // (values.shape[position] // parts)).reshape([-1 if axis == position else 1 for axis in range(values.ndim)]) for position in (source, target)]
    chosen = jax.random.permutation(rng, parts)[partner]
    strong = (owner == chosen) | (owner == (partner + parts // 2) % parts)
    return jnp.where(strong, factor * values, values)


def block_levels(stream_key, extent, cuts, least, largest):
    factor_of, own = 1.0, jax.random.fold_in(stream_key, 6)
    for position, parts in cuts:
        heights = jnp.exp(jax.random.uniform(jax.random.fold_in(own, position), (parts,), jnp.float32, least / len(cuts), largest / len(cuts)))
        factor_of = factor_of * jnp.repeat(heights, extent[position] // parts).reshape([-1 if axis == position else 1 for axis in range(len(extent))])
    return factor_of


def normal_values(rng, extent, scale, most, pieces=(), held_as=jnp.bfloat16):
    entries = jax.random.normal(rng, extent, jnp.float32) * scale
    if len(pieces) > 0:
        entries = block_levels(rng, extent, pieces, -0.22, 0.18) * entries
    return jnp.clip(entries, min=-most, max=most).astype(held_as)


def bell_draw_with(own_key, extent, scale, limit, shards, heavy, held_as=jnp.bfloat16):
    array = scale * jax.random.normal(own_key, extent, jnp.float32)
    if shards:
        array = array * block_levels(own_key, extent, shards, -0.22, 0.18)
    return jnp.clip(spiked(array, jax.random.fold_in(own_key, 3), *heavy), -limit, limit).astype(held_as)


def setup_inputs(seed: int = 0, part: int = 0) -> dict:
    key_list = jax.random.split(jax.random.key(seed), 6)
    part_keys = jax.random.split(jax.random.fold_in(key_list[5], part), 6)
    features = normal_values(part_keys[0], (LENGTH, D), 1.0, 6.0, ((0, 4), (1, 4)))
    filter_taps = normal_values(key_list[1], (LENGTH, D), LENGTH ** -0.5, 0.125, ((1, 4),))
    skip_gain = normal_values(key_list[2], (D,), 1.0, 4.0, ((0, 4),), jnp.float32)
    in_weight = normal_values(key_list[3], (D, 3, D), D ** -0.5, 0.09375, ((2, 4),))
    out_weight = bell_draw_with(key_list[4], (D, D), D ** -0.5, 0.125, ((1, 4),), (0, 1, 4, 2.0))
    return dict(features=features, filter_taps=filter_taps, skip_gain=skip_gain, in_weight=in_weight, out_weight=out_weight)


def dft_tables(block_len):
    period = 2 * block_len
    freq_col = jnp.arange(period, dtype=jnp.int32)[:, None]
    place_row = jnp.arange(period, dtype=jnp.int32)[None, :]
    angles = ((freq_col * place_row) % period).astype(jnp.float32) * (2.0 * math.pi / period)
    forward = jnp.concatenate([jnp.cos(angles), -jnp.sin(angles)], axis=0).astype(jnp.bfloat16)
    out_place = jnp.arange(block_len, dtype=jnp.int32)[:, None] + block_len
    angle_out = ((out_place * place_row) % period).astype(jnp.float32) * (2.0 * math.pi / period)
    inverse = (jnp.concatenate([jnp.cos(angle_out), -jnp.sin(angle_out)], axis=1) / period).astype(jnp.bfloat16)
    return forward, inverse


def reference(features, filter_taps, skip_gain, in_weight, out_weight):
    blocks = LENGTH // P_SIZE
    period = 2 * P_SIZE
    highest = lax.Precision.HIGHEST
    forward, inverse = dft_tables(P_SIZE)
    projected = jnp.dot(features, in_weight.reshape(D, 3 * D), preferred_element_type=jnp.float32)
    query_rows = projected[:, :D].astype(jnp.bfloat16)
    mixed_in = (projected[:, D:2 * D] * projected[:, 2 * D:]).astype(jnp.bfloat16)
    kv_blocks = mixed_in.reshape(blocks, P_SIZE, D).astype(jnp.float32)
    input_spectra = jnp.einsum('fp,bpd->bfd', forward[:, :P_SIZE].astype(jnp.float32), kv_blocks, precision=highest).astype(jnp.bfloat16)
    padded = jnp.concatenate([jnp.zeros((P_SIZE, D), jnp.bfloat16), filter_taps], axis=0)
    tap_blocks = padded.reshape(blocks + 1, P_SIZE, D)
    segments = jnp.concatenate([tap_blocks[:-1], tap_blocks[1:]], axis=1).astype(jnp.float32)
    lag_spectra = jnp.einsum('fn,knd->kfd', forward.astype(jnp.float32), segments, precision=highest).astype(jnp.bfloat16)
    flipped = jnp.concatenate([lag_spectra[::-1], jnp.zeros_like(lag_spectra)], axis=0)
    source = input_spectra.astype(jnp.float32)
    source_re = source[:, :period]
    source_im = source[:, period:]

    def one_block(out_block):
        window = lax.dynamic_slice_in_dim(flipped, (blocks - 1 - out_block).astype(jnp.int32), blocks, 0).astype(jnp.float32)
        lag_re = window[:, :period]
        lag_im = window[:, period:]
        out_re = jnp.sum(lag_re * source_re - lag_im * source_im, axis=0)
        out_im = jnp.sum(lag_re * source_im + lag_im * source_re, axis=0)
        return jnp.concatenate([out_re, out_im], axis=0).astype(jnp.bfloat16)

    block_spectra = lax.map(one_block, jnp.arange(blocks, dtype=jnp.int32))
    conv_out = jnp.einsum('tf,bfd->btd', inverse.astype(jnp.float32), block_spectra.astype(jnp.float32), precision=highest).reshape(LENGTH, D)
    gated_rows = (query_rows.astype(jnp.float32) * (conv_out + skip_gain[None, :] * mixed_in.astype(jnp.float32))).astype(jnp.bfloat16)
    return jnp.dot(gated_rows, out_weight, preferred_element_type=jnp.float32).astype(jnp.bfloat16)
```

```python
import functools
import math

import jax
import jax.numpy as jnp
import numpy as np
from jax import lax
from jax.experimental import pallas as pl
from jax.experimental.pallas import tpu as pltpu
from jax.sharding import PartitionSpec as P

BLOCK = 256


def tables(block):
    period = 2 * block
    freq = 2 * np.arange(block, dtype=np.int64)[:, None] + 1
    place = np.arange(period, dtype=np.int64)[None, :]
    angle = (freq * place % (2 * period)) * (math.pi / period)
    forward = np.concatenate([np.cos(angle), -np.sin(angle)], axis=0)
    kept = angle[:, block:].T
    inverse = np.concatenate([np.cos(kept), -np.sin(kept)], axis=1) / block
    return jnp.asarray(forward, jnp.bfloat16), jnp.asarray(inverse, jnp.bfloat16)


def conv_kernel(n, x_ref, taps_ref, skip_ref, fwd_ref, inv_ref, out_ref, xs, gs, ys):
    me = lax.axis_index("ctx")
    rows, cc = x_ref.shape[1], x_ref.shape[2]
    per = rows // BLOCK
    blocks = n * per
    for k in range(blocks):
        if k == 0:
            gs[k] = jnp.dot(fwd_ref[:, BLOCK:], taps_ref[:BLOCK], preferred_element_type=jnp.float32)
        else:
            gs[k] = jnp.dot(
                fwd_ref[...], taps_ref[(k - 1) * BLOCK : (k + 1) * BLOCK], preferred_element_type=jnp.float32
            )
    for a in range(blocks):
        slot = lax.rem(me - a // per + n, n)
        part = slice((a % per) * BLOCK, (a % per + 1) * BLOCK)
        xs[a] = jnp.dot(fwd_ref[:, :BLOCK], x_ref[slot, part, :], preferred_element_type=jnp.float32)

    lane = min(cc, 128)

    def mix(i, carry):
        re = pl.ds(pl.multiple_of(i * 8, 8), 8)
        im = pl.ds(pl.multiple_of(i * 8 + BLOCK, 8), 8)
        for l in range(0, cc, lane):
            ls = slice(l, l + lane)
            xr = [xs[a, re, ls] for a in range(blocks)]
            xi = [xs[a, im, ls] for a in range(blocks)]
            gr = [gs[a, re, ls] for a in range(blocks)]
            gi = [gs[a, im, ls] for a in range(blocks)]
            for b in range(blocks):
                yr = xr[0] * gr[b] - xi[0] * gi[b]
                yi = xi[0] * gr[b] + xr[0] * gi[b]
                for a in range(1, b + 1):
                    yr = yr + xr[a] * gr[b - a] - xi[a] * gi[b - a]
                    yi = yi + xi[a] * gr[b - a] + xr[a] * gi[b - a]
                ys[b, re, ls] = yr
                ys[b, im, ls] = yi
        return carry

    lax.fori_loop(0, BLOCK // 8, mix, 0)
    for b in range(blocks):
        owner = b // per
        part = slice((b % per) * BLOCK, (b % per + 1) * BLOCK)
        conv = jnp.dot(inv_ref[...], ys[b].astype(jnp.bfloat16), preferred_element_type=jnp.float32)
        held = x_ref[lax.rem(me - owner + n, n), part, :].astype(jnp.float32)
        out_ref[lax.rem(owner - me + n, n), part, :] = (conv + skip_ref[...] * held).astype(jnp.bfloat16)


def convolve(n, x, taps, skip):
    rows, cc = x.shape[1:]
    forward, inverse = tables(BLOCK)
    blocks = n * rows // BLOCK
    spectra = pltpu.VMEM((blocks, 2 * BLOCK, cc), jnp.float32)
    return pl.pallas_call(
        functools.partial(conv_kernel, n),
        out_shape=jax.ShapeDtypeStruct(x.shape, jnp.bfloat16),
        in_specs=[pl.BlockSpec(memory_space=pltpu.VMEM)] * 5,
        out_specs=pl.BlockSpec(memory_space=pltpu.VMEM),
        scratch_shapes=[spectra, spectra, spectra],
        compiler_params=pltpu.CompilerParams(vmem_limit_bytes=40 * 1024 * 1024),
        cost_estimate=pl.CostEstimate(flops=8_000_000_000, bytes_accessed=4_000_000, transcendentals=0),
    )(x, taps, skip, forward, inverse)


def shift(x, axis, n, by):
    return lax.ppermute(x, axis, [(i, (i + by) % n) for i in range(n)])


def flip(x, n, bit):
    return lax.ppermute(x, "chan", [(i, i ^ bit) for i in range(n)])


def gather_pieces(x, n):
    across = flip(x, n, 2)
    beside = flip(x, n, 1)
    return [(0, x), (1, beside), (2, across), (3, flip(across, n, 1))]


def gather(x, n):
    if n != 4:
        return lax.all_gather(x, "chan", axis=1, tiled=True)
    me = lax.axis_index("chan")
    width = x.shape[1]
    whole = jnp.zeros((x.shape[0], n * width), x.dtype)
    for far, piece in gather_pieces(x, n):
        whole = lax.dynamic_update_slice(whole, piece, (0, (me ^ far) * width))
    return whole


def exchange(parts, n):
    return [parts[0]] + [shift(parts[s], "ctx", n, s) for s in range(1, n)]


def shards(features, filter_taps, skip_gain, in_weight, out_weight):
    f32 = jnp.float32
    n_ctx, n_chan = lax.axis_size("ctx"), lax.axis_size("chan")
    ctx, chan = lax.axis_index("ctx"), lax.axis_index("chan")
    rows, channels = features.shape[0], in_weight.shape[2]
    cc = channels // n_ctx
    taps = lax.dynamic_slice_in_dim(filter_taps, ctx * cc, cc, 1)
    skip = lax.dynamic_slice_in_dim(skip_gain, ctx * cc, cc, 0)[None, :]

    whole = gather(features, n_chan)
    key = jnp.dot(whole, in_weight[:, 1], preferred_element_type=f32)
    value = jnp.dot(whole, in_weight[:, 2], preferred_element_type=f32)
    mixed = (key * value).astype(jnp.bfloat16)
    sends = [
        lax.dynamic_slice_in_dim(mixed, ((ctx + s) % n_ctx) * cc, cc, 1) for s in range(n_ctx)
    ]
    x = jnp.stack(exchange(sends, n_ctx))
    query = jnp.dot(whole, in_weight[:, 0], preferred_element_type=f32).astype(jnp.bfloat16)
    y = convolve(n_ctx, x, taps, skip)
    back = exchange([y[s] for s in range(n_ctx)], n_ctx)
    summed = jnp.zeros((rows, channels), jnp.bfloat16)
    for s in range(n_ctx):
        summed = lax.dynamic_update_slice(summed, back[s], (0, ((ctx - s + n_ctx) % n_ctx) * cc))
    gated = (query.astype(f32) * summed.astype(f32)).astype(jnp.bfloat16)
    if n_chan != 4:
        return jnp.dot(gather(gated, n_chan), out_weight, preferred_element_type=f32).astype(jnp.bfloat16)
    total = None
    for far, piece in gather_pieces(gated, n_chan):
        weight = lax.dynamic_slice_in_dim(out_weight, (chan ^ far) * channels, channels, 0)
        term = jnp.dot(piece, weight, preferred_element_type=f32)
        total = term if total is None else total + term
    return total.astype(jnp.bfloat16)


def solution(mesh):
    return jax.shard_map(
        shards,
        mesh=mesh,
        in_specs=(
            P(("grp", "ctx"), "chan"),
            P(None, "chan"),
            P("chan"),
            P(None, None, "chan"),
            P(None, "chan"),
        ),
        out_specs=P(("grp", "ctx"), "chan"),
        check_vma=False,
    )
```

```python
import functools
import math

import jax
import jax.numpy as jnp
import numpy as np
from jax import lax
from jax.experimental import pallas as pl
from jax.experimental.pallas import tpu as pltpu
from jax.sharding import PartitionSpec as P

BLOCK = 256


def tables(block):
    period = 2 * block
    freq = 2 * np.arange(block, dtype=np.int64)[:, None] + 1
    place = np.arange(period, dtype=np.int64)[None, :]
    angle = (freq * place % (2 * period)) * (math.pi / period)
    forward = np.concatenate([np.cos(angle), -np.sin(angle)], axis=0)
    kept = angle[:, block:].T
    inverse = np.concatenate([np.cos(kept), -np.sin(kept)], axis=1) / block
    return jnp.asarray(forward, jnp.bfloat16), jnp.asarray(inverse, jnp.bfloat16)


def conv_kernel(n, per, *refs):
    count = n * per
    x_refs, (taps_ref, skip_ref, fwd_ref, inv_ref) = refs[:count], refs[count : count + 4]
    out_refs, (xs, gs, ys) = refs[count + 4 : 2 * count + 4], refs[2 * count + 4 :]
    me = lax.axis_index("ctx")
    cc = taps_ref.shape[1]
    for k in range(count):
        if k == 0:
            gs[k] = jnp.dot(fwd_ref[:, BLOCK:], taps_ref[:BLOCK], preferred_element_type=jnp.float32)
        else:
            gs[k] = jnp.dot(
                fwd_ref[...], taps_ref[(k - 1) * BLOCK : (k + 1) * BLOCK], preferred_element_type=jnp.float32
            )
    for s in range(n):
        for t in range(per):
            xs[lax.rem(me - s + n, n) * per + t] = jnp.dot(
                fwd_ref[:, :BLOCK], x_refs[s * per + t][...], preferred_element_type=jnp.float32
            )

    lane = min(cc, 128)

    def mix(i, carry):
        re = pl.ds(pl.multiple_of(i * 8, 8), 8)
        im = pl.ds(pl.multiple_of(i * 8 + BLOCK, 8), 8)
        for l in range(0, cc, lane):
            ls = slice(l, l + lane)
            xr = [xs[a, re, ls] for a in range(count)]
            xi = [xs[a, im, ls] for a in range(count)]
            gr = [gs[a, re, ls] for a in range(count)]
            gi = [gs[a, im, ls] for a in range(count)]
            for b in range(count):
                yr = xr[0] * gr[b] - xi[0] * gi[b]
                yi = xi[0] * gr[b] + xr[0] * gi[b]
                for a in range(1, b + 1):
                    yr = yr + xr[a] * gr[b - a] - xi[a] * gi[b - a]
                    yi = yi + xi[a] * gr[b - a] + xr[a] * gi[b - a]
                ys[b, re, ls] = yr
                ys[b, im, ls] = yi
        return carry

    lax.fori_loop(0, BLOCK // 8, mix, 0)
    for s in range(n):
        for t in range(per):
            spectra = ys[lax.rem(me + s, n) * per + t].astype(jnp.bfloat16)
            conv = jnp.dot(inv_ref[...], spectra, preferred_element_type=jnp.float32)
            held = x_refs[(n - s) % n * per + t][...].astype(jnp.float32)
            out_refs[s * per + t][...] = (conv + skip_ref[...] * held).astype(jnp.bfloat16)


def convolve(n, per, x, taps, skip):
    cc = taps.shape[1]
    forward, inverse = tables(BLOCK)
    count = n * per
    spectra = pltpu.VMEM((count, 2 * BLOCK, cc), jnp.float32)
    vmem = pl.BlockSpec(memory_space=pltpu.VMEM)
    return pl.pallas_call(
        functools.partial(conv_kernel, n, per),
        out_shape=[jax.ShapeDtypeStruct((BLOCK, cc), jnp.bfloat16)] * count,
        in_specs=[vmem] * (count + 4),
        out_specs=[vmem] * count,
        scratch_shapes=[spectra, spectra, spectra],
        compiler_params=pltpu.CompilerParams(vmem_limit_bytes=40 * 1024 * 1024),
        cost_estimate=pl.CostEstimate(flops=6_000_000_000, bytes_accessed=4_000_000, transcendentals=0),
    )(*x, taps, skip, forward, inverse)


def shift(x, axis, n, by):
    return lax.ppermute(x, axis, [(i, (i + by) % n) for i in range(n)])


def flip(x, n, bit):
    return lax.ppermute(x, "chan", [(i, i ^ bit) for i in range(n)])


def after(x, *others):
    return lax.optimization_barrier((x, *others))[0]


def exchange(parts, n):
    return [parts[0]] + [shift(parts[s], "ctx", n, s) for s in range(1, n)]


def shards(features, filter_taps, skip_gain, in_weight, out_weight):
    f32 = jnp.float32
    n_ctx, n_chan = lax.axis_size("ctx"), lax.axis_size("chan")
    ctx, chan = lax.axis_index("ctx"), lax.axis_index("chan")
    rows, channels = features.shape[0], in_weight.shape[2]
    width = features.shape[1]
    cc = channels // n_ctx
    per = rows // BLOCK
    paired = n_chan == 4
    taps = lax.dynamic_slice_in_dim(filter_taps, ctx * cc, cc, 1)
    skip = lax.dynamic_slice_in_dim(skip_gain, ctx * cc, cc, 0)[None, :]
    parts = range(per)

    def into(piece, owner, s):
        weight = lax.dynamic_slice(in_weight, (owner * width, s, 0), (width, 1, channels))[:, 0]
        return jnp.dot(piece, weight, preferred_element_type=f32)

    def chunk(x, t):
        return x[t * BLOCK : (t + 1) * BLOCK]

    if paired:
        across, last = [], None
        for t in parts:
            sent = chunk(features, t)
            across.append(flip(sent if last is None else after(sent, last), n_chan, 2))
            last = across[-1]
        beside = flip(features, n_chan, 1)
        near = [into(features, chan, s) + into(beside, chan ^ 1, s) for s in range(3)]
        far = [[(chan ^ 2, across[t]), (chan ^ 3, flip(across[t], n_chan, 1))] for t in parts]
    else:
        whole = lax.all_gather(features, "chan", axis=1, tiled=True)
        near = [into(whole[:, :width], 0, s) for s in range(3)]
        far = [[(j, chunk(whole, t)[:, j * width : (j + 1) * width]) for j in range(1, n_chan)] for t in parts]

    def project(t, s):
        total = chunk(near[s], t)
        for owner, piece in far[t]:
            total = total + into(piece, owner, s)
        return total

    got = []
    for t in parts:
        mixed = (project(t, 1) * project(t, 2)).astype(jnp.bfloat16)
        sends = [
            lax.dynamic_slice_in_dim(mixed, ((ctx + s) % n_ctx) * cc, cc, 1) for s in range(n_ctx)
        ]
        got.append(exchange(sends, n_ctx))
    query = [project(t, 0).astype(jnp.bfloat16) for t in parts]
    x = [got[t][s] for s in range(n_ctx) for t in parts]
    x = lax.optimization_barrier((*x, *query))[: len(x)]
    y = convolve(n_ctx, per, x, taps, skip)

    outs, last = [], None
    for t in parts:
        sends = [y[s * per + t] for s in range(n_ctx)]
        if last is not None:
            sends = lax.optimization_barrier((*sends, *last))[:n_ctx]
        back = last = exchange(sends, n_ctx)
        summed = jnp.zeros((BLOCK, channels), jnp.bfloat16)
        for s in range(n_ctx):
            summed = lax.dynamic_update_slice(summed, back[s], (0, ((ctx - s + n_ctx) % n_ctx) * cc))
        gated = (query[t].astype(f32) * summed.astype(f32)).astype(jnp.bfloat16)
        if paired:
            far_side = flip(gated, n_chan, 2)
            pieces = [(chan, gated), (chan ^ 1, flip(gated, n_chan, 1))]
            pieces += [(chan ^ 2, far_side), (chan ^ 3, flip(far_side, n_chan, 1))]
        else:
            pieces = [(0, lax.all_gather(gated, "chan", axis=1, tiled=True))]
        total = None
        for owner, piece in pieces:
            depth = piece.shape[1]
            weight = lax.dynamic_slice_in_dim(out_weight, owner * depth, depth, 0)
            term = jnp.dot(piece, weight, preferred_element_type=f32)
            total = term if total is None else total + term
        outs.append(total.astype(jnp.bfloat16))
    return jnp.concatenate(outs, axis=0)


def solution(mesh):
    return jax.shard_map(
        shards,
        mesh=mesh,
        in_specs=(
            P(("grp", "ctx"), "chan"),
            P(None, "chan"),
            P("chan"),
            P(None, None, "chan"),
            P(None, "chan"),
        ),
        out_specs=P(("grp", "ctx"), "chan"),
        check_vma=False,
    )
```

```python
import functools
import math

import jax
import jax.numpy as jnp
import numpy as np
from jax import lax
from jax.experimental import pallas as pl
from jax.experimental.pallas import tpu as pltpu
from jax.sharding import PartitionSpec as P

BLOCK = 256


def tables(block):
    period = 2 * block
    freq = 2 * np.arange(block, dtype=np.int64)[:, None] + 1
    place = np.arange(period, dtype=np.int64)[None, :]
    angle = (freq * place % (2 * period)) * (math.pi / period)
    forward = np.concatenate([np.cos(angle), -np.sin(angle)], axis=0)
    kept = angle[:, block:].T
    inverse = np.concatenate([np.cos(kept), -np.sin(kept)], axis=1) / block
    return jnp.asarray(forward, jnp.bfloat16), jnp.asarray(inverse, jnp.bfloat16)


def conv_kernel(n, per, *refs):
    count = n * per
    x_refs, (taps_ref, skip_ref, fwd_ref, inv_ref) = refs[:count], refs[count : count + 4]
    out_refs, (xs, gs, ys) = refs[count + 4 : 2 * count + 4], refs[2 * count + 4 :]
    me = lax.axis_index("ctx")
    cc = taps_ref.shape[1]
    for k in range(count):
        if k == 0:
            gs[k] = jnp.dot(fwd_ref[:, BLOCK:], taps_ref[:BLOCK], preferred_element_type=jnp.float32)
        else:
            gs[k] = jnp.dot(
                fwd_ref[...], taps_ref[(k - 1) * BLOCK : (k + 1) * BLOCK], preferred_element_type=jnp.float32
            )
    for s in range(n):
        for t in range(per):
            xs[lax.rem(me - s + n, n) * per + t] = jnp.dot(
                fwd_ref[:, :BLOCK], x_refs[s * per + t][...], preferred_element_type=jnp.float32
            )

    lane = min(cc, 128)

    def mix(i, carry):
        re = pl.ds(pl.multiple_of(i * 8, 8), 8)
        im = pl.ds(pl.multiple_of(i * 8 + BLOCK, 8), 8)
        for l in range(0, cc, lane):
            ls = slice(l, l + lane)
            xr = [xs[a, re, ls] for a in range(count)]
            xi = [xs[a, im, ls] for a in range(count)]
            gr = [gs[a, re, ls] for a in range(count)]
            gi = [gs[a, im, ls] for a in range(count)]
            for b in range(count):
                yr = xr[0] * gr[b] - xi[0] * gi[b]
                yi = xi[0] * gr[b] + xr[0] * gi[b]
                for a in range(1, b + 1):
                    yr = yr + xr[a] * gr[b - a] - xi[a] * gi[b - a]
                    yi = yi + xi[a] * gr[b - a] + xr[a] * gi[b - a]
                ys[b, re, ls] = yr
                ys[b, im, ls] = yi
        return carry

    lax.fori_loop(0, BLOCK // 8, mix, 0)
    for s in range(n):
        for t in range(per):
            spectra = ys[lax.rem(me + s, n) * per + t].astype(jnp.bfloat16)
            conv = jnp.dot(inv_ref[...], spectra, preferred_element_type=jnp.float32)
            held = x_refs[(n - s) % n * per + t][...].astype(jnp.float32)
            out_refs[s * per + t][...] = (conv + skip_ref[...] * held).astype(jnp.bfloat16)


def project_kernel(mats, ops, mode, *refs):
    refs = refs[1:]
    pieces, weights = refs[:ops], refs[ops : ops + ops * mats]
    outs = refs[ops + ops * mats :]
    sums = []
    for m in range(mats):
        total = outs[m][0] if mode != "near" else None
        for p in range(ops):
            term = jnp.dot(pieces[p][...], weights[m * ops + p][0], preferred_element_type=jnp.float32)
            total = term if total is None else total + term
        sums.append(total)
    if mode == "near":
        for m in range(mats):
            outs[m][0] = sums[m]

        @pl.when(pl.program_id(0) == 0)
        def _():
            outs[mats][...] = pieces[0][BLOCK:]
    elif mode == "mix":
        outs[mats][0] = (sums[0] * sums[1]).astype(jnp.bfloat16)
    else:
        outs[mats][0] = sums[0].astype(jnp.bfloat16)


def project(mode, where, pieces, distances, weight, mats, near, t, n):
    rows, width = pieces[0].shape
    channels = weight.shape[2]
    cc = channels // n

    def weight_spec(mat, far):
        return pl.BlockSpec((1, width, cc), lambda s, at: (mat, at[1] ^ far, lax.rem(at[0] + s, n)))

    specs = [pl.BlockSpec((rows, width), lambda s, at: (0, 0))] * len(pieces)
    specs += [weight_spec(mat, far) for mat in mats for far in distances]
    specs += [pl.BlockSpec((1, rows, cc), lambda s, at: (s, t, 0))] * len(near)
    out_spec = pl.BlockSpec((1, rows, cc), lambda s, at: (s, 0, 0))
    if mode == "near":
        shapes = [jax.ShapeDtypeStruct((n, rows, cc), jnp.float32)] * len(mats)
        later = jax.ShapeDtypeStruct((rows - BLOCK, width), jnp.bfloat16)
    else:
        shapes = [jax.ShapeDtypeStruct((n, rows, cc), jnp.bfloat16)]
        later = None
    out_specs = [out_spec] * len(shapes)
    if later is not None:
        shapes.append(later)
        out_specs.append(pl.BlockSpec(later.shape, lambda s, at: (0, 0)))
    flops = 2 * rows * width * channels * len(pieces) * len(mats)
    return pl.pallas_call(
        functools.partial(project_kernel, len(mats), len(pieces), mode),
        out_shape=shapes,
        grid_spec=pltpu.PrefetchScalarGridSpec(
            num_scalar_prefetch=1, grid=(n,), in_specs=specs, out_specs=out_specs
        ),
        compiler_params=pltpu.CompilerParams(vmem_limit_bytes=36 * 1024 * 1024),
        cost_estimate=pl.CostEstimate(flops=flops, bytes_accessed=flops // rows, transcendentals=0),
    )(where, *pieces, *([weight] * (len(mats) * len(distances))), *near)


def convolve(n, per, x, taps, skip):
    cc = taps.shape[1]
    forward, inverse = tables(BLOCK)
    count = n * per
    spectra = pltpu.VMEM((count, 2 * BLOCK, cc), jnp.float32)
    vmem = pl.BlockSpec(memory_space=pltpu.VMEM)
    return pl.pallas_call(
        functools.partial(conv_kernel, n, per),
        out_shape=[jax.ShapeDtypeStruct((BLOCK, cc), jnp.bfloat16)] * count,
        in_specs=[vmem] * (count + 4),
        out_specs=[vmem] * count,
        scratch_shapes=[spectra, spectra, spectra],
        compiler_params=pltpu.CompilerParams(vmem_limit_bytes=40 * 1024 * 1024),
        cost_estimate=pl.CostEstimate(flops=6_000_000_000, bytes_accessed=4_000_000, transcendentals=0),
    )(*x, taps, skip, forward, inverse)


def shift(x, axis, n, by):
    return lax.ppermute(x, axis, [(i, (i + by) % n) for i in range(n)])


def flip(x, n, bit):
    return lax.ppermute(x, "chan", [(i, i ^ bit) for i in range(n)])


def after(x, *others):
    return lax.optimization_barrier((x, *others))[0]


def exchange(parts, n):
    return [parts[0]] + [shift(parts[s], "ctx", n, s) for s in range(1, n)]


def shards(features, filter_taps, skip_gain, in_weight, out_weight):
    f32 = jnp.float32
    n_ctx, n_chan = lax.axis_size("ctx"), lax.axis_size("chan")
    ctx, chan = lax.axis_index("ctx"), lax.axis_index("chan")
    rows, channels = features.shape[0], in_weight.shape[2]
    cc = channels // n_ctx
    per = rows // BLOCK
    paired = n_chan == 4
    taps = lax.dynamic_slice_in_dim(filter_taps, ctx * cc, cc, 1)
    skip = lax.dynamic_slice_in_dim(skip_gain, ctx * cc, cc, 0)[None, :]
    parts = range(per)

    def chunk(x, t):
        return x[t * BLOCK : (t + 1) * BLOCK]

    got, query = [], []
    if paired and cc % 128 == 0:
        where = jnp.stack([ctx, chan]).astype(jnp.int32)
        weight = jnp.transpose(in_weight, (1, 0, 2))
        first = flip(chunk(features, 0), n_chan, 2)
        beside = flip(features, n_chan, 1)
        *near, later = project("near", where, [features, beside], (0, 1), weight, (1, 2, 0), [], 0, n_ctx)
        across = [first]
        for t in parts[1:]:
            across.append(flip(after(chunk(later, t - 1), across[-1]), n_chan, 2))
        far = [[across[t], flip(across[t], n_chan, 1)] for t in parts]
        for t in parts:
            mixed = project("mix", where, far[t], (2, 3), weight, (1, 2), near[:2], t, n_ctx)[0]
            got.append(exchange([mixed[s] for s in range(n_ctx)], n_ctx))
        held = got[-1][0]
        for t in parts:
            pieces = lax.optimization_barrier((*far[t], held))[:2]
            query.append(project("query", where, pieces, (2, 3), weight, (0,), near[2:], t, n_ctx)[0])
    else:
        whole = lax.all_gather(features, "chan", axis=1, tiled=True)
        turned = [jnp.roll(in_weight[:, s], -ctx * cc, axis=1) for s in range(3)]
        for t in parts:
            q, k, v = [jnp.dot(chunk(whole, t), w, preferred_element_type=f32) for w in turned]
            mixed = (k * v).astype(jnp.bfloat16)
            got.append(exchange([mixed[:, s * cc : (s + 1) * cc] for s in range(n_ctx)], n_ctx))
            q = q.astype(jnp.bfloat16)
            query.append(jnp.stack([q[:, s * cc : (s + 1) * cc] for s in range(n_ctx)]))
    x = [got[t][s] for s in range(n_ctx) for t in parts]
    x = lax.optimization_barrier((*x, *query))[: len(x)]
    y = convolve(n_ctx, per, x, taps, skip)

    outs, last = [], None
    for t in parts:
        sends = [y[s * per + t] for s in range(n_ctx)]
        if last is not None:
            sends = lax.optimization_barrier((*sends, *last))[:n_ctx]
        back = last = exchange(sends, n_ctx)
        gated = jnp.zeros((BLOCK, channels), jnp.bfloat16)
        for s in range(n_ctx):
            piece = query[t][(n_ctx - s) % n_ctx].astype(f32) * back[s].astype(f32)
            start = ((ctx - s + n_ctx) % n_ctx) * cc
            gated = lax.dynamic_update_slice(gated, piece.astype(jnp.bfloat16), (0, start))
        if paired:
            far_side = flip(gated, n_chan, 2)
            pieces = [(chan, gated), (chan ^ 1, flip(gated, n_chan, 1))]
            pieces += [(chan ^ 2, far_side), (chan ^ 3, flip(far_side, n_chan, 1))]
        else:
            pieces = [(0, lax.all_gather(gated, "chan", axis=1, tiled=True))]
        total = None
        for owner, piece in pieces:
            depth = piece.shape[1]
            weight = lax.dynamic_slice_in_dim(out_weight, owner * depth, depth, 0)
            term = jnp.dot(piece, weight, preferred_element_type=f32)
            total = term if total is None else total + term
        outs.append(total.astype(jnp.bfloat16))
    return jnp.concatenate(outs, axis=0)


def solution(mesh):
    return jax.shard_map(
        shards,
        mesh=mesh,
        in_specs=(
            P(("grp", "ctx"), "chan"),
            P(None, "chan"),
            P("chan"),
            P(None, None, "chan"),
            P(None, "chan"),
        ),
        out_specs=P(("grp", "ctx"), "chan"),
        check_vma=False,
    )
```

```python
import functools
import math

import jax
import jax.numpy as jnp
import numpy as np
from jax import lax
from jax.experimental import pallas as pl
from jax.experimental.pallas import tpu as pltpu
from jax.sharding import PartitionSpec as P

BLOCK = 256


def tables(block):
    period = 2 * block
    freq = 2 * np.arange(block, dtype=np.int64)[:, None] + 1
    place = np.arange(period, dtype=np.int64)[None, :]
    angle = (freq * place % (2 * period)) * (math.pi / period)
    forward = np.concatenate([np.cos(angle), -np.sin(angle)], axis=0)
    kept = angle[:, block:].T
    inverse = np.concatenate([np.cos(kept), -np.sin(kept)], axis=1) / block
    return jnp.asarray(forward, jnp.bfloat16), jnp.asarray(inverse, jnp.bfloat16)


def conv_kernel(n, per, *refs):
    count = n * per
    x_refs, (taps_ref, skip_ref, fwd_ref, inv_ref) = refs[:count], refs[count : count + 4]
    out_refs, (xs, gs, ys) = refs[count + 4 : 2 * count + 4], refs[2 * count + 4 :]
    me = lax.axis_index("ctx")
    cc = taps_ref.shape[1]
    for k in range(count):
        if k == 0:
            gs[k] = jnp.dot(fwd_ref[:, BLOCK:], taps_ref[:BLOCK], preferred_element_type=jnp.float32)
        else:
            gs[k] = jnp.dot(
                fwd_ref[...], taps_ref[(k - 1) * BLOCK : (k + 1) * BLOCK], preferred_element_type=jnp.float32
            )
    for s in range(n):
        for t in range(per):
            xs[lax.rem(me - s + n, n) * per + t] = jnp.dot(
                fwd_ref[:, :BLOCK], x_refs[s * per + t][...], preferred_element_type=jnp.float32
            )

    lane = min(cc, 128)

    def mix(i, carry):
        re = pl.ds(pl.multiple_of(i * 8, 8), 8)
        im = pl.ds(pl.multiple_of(i * 8 + BLOCK, 8), 8)
        for l in range(0, cc, lane):
            ls = slice(l, l + lane)
            xr = [xs[a, re, ls] for a in range(count)]
            xi = [xs[a, im, ls] for a in range(count)]
            gr = [gs[a, re, ls] for a in range(count)]
            gi = [gs[a, im, ls] for a in range(count)]
            for b in range(count):
                yr = xr[0] * gr[b] - xi[0] * gi[b]
                yi = xi[0] * gr[b] + xr[0] * gi[b]
                for a in range(1, b + 1):
                    yr = yr + xr[a] * gr[b - a] - xi[a] * gi[b - a]
                    yi = yi + xi[a] * gr[b - a] + xr[a] * gi[b - a]
                ys[b, re, ls] = yr
                ys[b, im, ls] = yi
        return carry

    lax.fori_loop(0, BLOCK // 8, mix, 0)
    for s in range(n):
        for t in range(per):
            spectra = ys[lax.rem(me + s, n) * per + t].astype(jnp.bfloat16)
            conv = jnp.dot(inv_ref[...], spectra, preferred_element_type=jnp.float32)
            held = x_refs[(n - s) % n * per + t][...].astype(jnp.float32)
            out_refs[s * per + t][...] = (conv + skip_ref[...] * held).astype(jnp.bfloat16)


def project_kernel(n, mats, ops, mode, where, *refs):
    pieces, weights = refs[:ops], refs[ops : ops + ops * mats]
    refs = refs[ops + ops * mats :]
    near, outs = (refs[:0], refs) if mode == "near" else (refs[:mats], refs[mats:])
    sums = outs[:mats] if mode == "near" else outs[1:]
    step = pl.program_id(0)

    @pl.when(step == 0)
    def _():
        for m in range(mats):
            sums[m][...] = jnp.zeros_like(sums[m]) if mode == "near" else near[m][...]

    for m in range(mats):
        total = sums[m][...]
        for p in range(ops):
            total = total + jnp.dot(
                pieces[p][...], weights[m * ops + p][0], preferred_element_type=jnp.float32
            )
        sums[m][...] = total

    if mode == "near":
        outs[mats][...] = pieces[0][BLOCK:]
    else:

        @pl.when(step == pl.num_programs(0) - 1)
        def _():
            cc = outs[0].shape[2]
            for j in range(n):
                ls = slice(j * cc, (j + 1) * cc)
                value = sums[0][:, ls] * sums[1][:, ls] if mode == "mix" else sums[0][:, ls]
                outs[0][lax.rem(j - where[0] + n, n)] = value.astype(jnp.bfloat16)


def project(mode, where, pieces, distances, weight, mats, near, t, n):
    rows, width = pieces[0].shape
    channels = weight.shape[2]
    depth = min(width, 256)
    steps = width // depth

    def weight_spec(mat, far):
        return pl.BlockSpec((1, depth, channels), lambda k, at: (mat, (at[1] ^ far) * steps + k, 0))

    specs = [pl.BlockSpec((rows, depth), lambda k, at: (0, k))] * len(pieces)
    specs += [weight_spec(mat, far) for mat in mats for far in distances]
    specs += [pl.BlockSpec((rows, channels), lambda k, at: (t, 0))] * len(near)
    total = (rows, channels)
    if mode == "near":
        shapes = [jax.ShapeDtypeStruct(total, jnp.float32)] * len(mats)
        shapes.append(jax.ShapeDtypeStruct((rows - BLOCK, width), jnp.bfloat16))
        out_specs = [pl.BlockSpec(total, lambda k, at: (0, 0))] * len(mats)
        out_specs.append(pl.BlockSpec((rows - BLOCK, depth), lambda k, at: (0, k)))
        scratch = []
    else:
        shapes = [jax.ShapeDtypeStruct((n, rows, channels // n), jnp.bfloat16)]
        out_specs = [pl.BlockSpec(shapes[0].shape, lambda k, at: (0, 0, 0))]
        scratch = [pltpu.VMEM(total, jnp.float32)] * len(mats)
    flops = 2 * rows * width * channels * len(pieces) * len(mats)
    return pl.pallas_call(
        functools.partial(project_kernel, n, len(mats), len(pieces), mode),
        out_shape=shapes,
        grid_spec=pltpu.PrefetchScalarGridSpec(
            num_scalar_prefetch=1, grid=(steps,), in_specs=specs, out_specs=out_specs, scratch_shapes=scratch
        ),
        compiler_params=pltpu.CompilerParams(vmem_limit_bytes=36 * 1024 * 1024),
        cost_estimate=pl.CostEstimate(flops=flops, bytes_accessed=flops // rows, transcendentals=0),
    )(where, *pieces, *([weight] * (len(mats) * len(distances))), *near)


def convolve(n, per, x, taps, skip):
    cc = taps.shape[1]
    forward, inverse = tables(BLOCK)
    count = n * per
    spectra = pltpu.VMEM((count, 2 * BLOCK, cc), jnp.float32)
    vmem = pl.BlockSpec(memory_space=pltpu.VMEM)
    return pl.pallas_call(
        functools.partial(conv_kernel, n, per),
        out_shape=[jax.ShapeDtypeStruct((BLOCK, cc), jnp.bfloat16)] * count,
        in_specs=[vmem] * (count + 4),
        out_specs=[vmem] * count,
        scratch_shapes=[spectra, spectra, spectra],
        compiler_params=pltpu.CompilerParams(vmem_limit_bytes=40 * 1024 * 1024),
        cost_estimate=pl.CostEstimate(flops=6_000_000_000, bytes_accessed=4_000_000, transcendentals=0),
    )(*x, taps, skip, forward, inverse)


def shift(x, axis, n, by):
    return lax.ppermute(x, axis, [(i, (i + by) % n) for i in range(n)])


def flip(x, n, bit):
    return lax.ppermute(x, "chan", [(i, i ^ bit) for i in range(n)])


def after(x, *others):
    return lax.optimization_barrier((x, *others))[0]


def exchange(parts, n):
    return [parts[0]] + [shift(parts[s], "ctx", n, s) for s in range(1, n)]


def shards(features, filter_taps, skip_gain, in_weight, out_weight):
    f32 = jnp.float32
    n_ctx, n_chan = lax.axis_size("ctx"), lax.axis_size("chan")
    ctx, chan = lax.axis_index("ctx"), lax.axis_index("chan")
    rows, channels = features.shape[0], in_weight.shape[2]
    cc = channels // n_ctx
    per = rows // BLOCK
    paired = n_chan == 4
    taps = lax.dynamic_slice_in_dim(filter_taps, ctx * cc, cc, 1)
    skip = lax.dynamic_slice_in_dim(skip_gain, ctx * cc, cc, 0)[None, :]
    parts = range(per)

    def chunk(x, t):
        return x[t * BLOCK : (t + 1) * BLOCK]

    got, query = [], []
    if paired and cc % 128 == 0:
        where = jnp.stack([ctx, chan]).astype(jnp.int32)
        weight = jnp.transpose(in_weight, (1, 0, 2))
        first = flip(chunk(features, 0), n_chan, 2)
        beside = flip(features, n_chan, 1)
        *near, later = project("near", where, [features, beside], (0, 1), weight, (1, 2, 0), [], 0, n_ctx)
        across = [first]
        for t in parts[1:]:
            across.append(flip(after(chunk(later, t - 1), across[-1]), n_chan, 2))
        far = [[across[t], flip(across[t], n_chan, 1)] for t in parts]
        for t in parts:
            mixed = project("mix", where, far[t], (2, 3), weight, (1, 2), near[:2], t, n_ctx)[0]
            got.append(exchange([mixed[s] for s in range(n_ctx)], n_ctx))
        held = got[-1][0]
        for t in parts:
            pieces = lax.optimization_barrier((*far[t], held))[:2]
            query.append(project("query", where, pieces, (2, 3), weight, (0,), near[2:], t, n_ctx)[0])
    else:
        whole = lax.all_gather(features, "chan", axis=1, tiled=True)
        turned = [jnp.roll(in_weight[:, s], -ctx * cc, axis=1) for s in range(3)]
        for t in parts:
            q, k, v = [jnp.dot(chunk(whole, t), w, preferred_element_type=f32) for w in turned]
            mixed = (k * v).astype(jnp.bfloat16)
            got.append(exchange([mixed[:, s * cc : (s + 1) * cc] for s in range(n_ctx)], n_ctx))
            q = q.astype(jnp.bfloat16)
            query.append(jnp.stack([q[:, s * cc : (s + 1) * cc] for s in range(n_ctx)]))
    x = [got[t][s] for s in range(n_ctx) for t in parts]
    x = lax.optimization_barrier((*x, *query))[: len(x)]
    y = convolve(n_ctx, per, x, taps, skip)

    outs, last = [], None
    for t in parts:
        sends = [y[s * per + t] for s in range(n_ctx)]
        if last is not None:
            sends = lax.optimization_barrier((*sends, *last))[:n_ctx]
        back = last = exchange(sends, n_ctx)
        gated = jnp.zeros((BLOCK, channels), jnp.bfloat16)
        for s in range(n_ctx):
            piece = query[t][(n_ctx - s) % n_ctx].astype(f32) * back[s].astype(f32)
            start = ((ctx - s + n_ctx) % n_ctx) * cc
            gated = lax.dynamic_update_slice(gated, piece.astype(jnp.bfloat16), (0, start))
        if paired:
            far_side = flip(gated, n_chan, 2)
            pieces = [(chan, gated), (chan ^ 1, flip(gated, n_chan, 1))]
            pieces += [(chan ^ 2, far_side), (chan ^ 3, flip(far_side, n_chan, 1))]
        else:
            pieces = [(0, lax.all_gather(gated, "chan", axis=1, tiled=True))]
        total = None
        for owner, piece in pieces:
            depth = piece.shape[1]
            weight = lax.dynamic_slice_in_dim(out_weight, owner * depth, depth, 0)
            term = jnp.dot(piece, weight, preferred_element_type=f32)
            total = term if total is None else total + term
        outs.append(total.astype(jnp.bfloat16))
    return jnp.concatenate(outs, axis=0)


def solution(mesh):
    return jax.shard_map(
        shards,
        mesh=mesh,
        in_specs=(
            P(("grp", "ctx"), "chan"),
            P(None, "chan"),
            P("chan"),
            P(None, None, "chan"),
            P(None, "chan"),
        ),
        out_specs=P(("grp", "ctx"), "chan"),
        check_vma=False,
    )
```

```python
import functools
import math

import jax
import jax.numpy as jnp
import numpy as np
from jax import lax
from jax.experimental import pallas as pl
from jax.experimental.pallas import tpu as pltpu
from jax.sharding import PartitionSpec as P

BLOCK = 256


def tables(block):
    period = 2 * block
    freq = 2 * np.arange(block, dtype=np.int64)[:, None] + 1
    place = np.arange(period, dtype=np.int64)[None, :]
    angle = (freq * place % (2 * period)) * (math.pi / period)
    forward = np.concatenate([np.cos(angle), -np.sin(angle)], axis=0)
    kept = angle[:, block:].T
    inverse = np.concatenate([np.cos(kept), -np.sin(kept)], axis=1) / block
    return jnp.asarray(forward, jnp.bfloat16), jnp.asarray(inverse, jnp.bfloat16)


def conv_kernel(n, per, *refs):
    count = n * per
    x_refs, (taps_ref, skip_ref, fwd_ref, inv_ref) = refs[:count], refs[count : count + 4]
    out_refs, (xs, gs, ys) = refs[count + 4 : 2 * count + 4], refs[2 * count + 4 :]
    me = lax.axis_index("ctx")
    cc = taps_ref.shape[1]
    for k in range(count):
        if k == 0:
            gs[k] = jnp.dot(fwd_ref[:, BLOCK:], taps_ref[:BLOCK], preferred_element_type=jnp.float32)
        else:
            gs[k] = jnp.dot(
                fwd_ref[...], taps_ref[(k - 1) * BLOCK : (k + 1) * BLOCK], preferred_element_type=jnp.float32
            )
    for s in range(n):
        for t in range(per):
            xs[lax.rem(me - s + n, n) * per + t] = jnp.dot(
                fwd_ref[:, :BLOCK], x_refs[s * per + t][...], preferred_element_type=jnp.float32
            )

    lane = min(cc, 128)

    def mix(i, carry):
        re = pl.ds(pl.multiple_of(i * 8, 8), 8)
        im = pl.ds(pl.multiple_of(i * 8 + BLOCK, 8), 8)
        for l in range(0, cc, lane):
            ls = slice(l, l + lane)
            xr = [xs[a, re, ls] for a in range(count)]
            xi = [xs[a, im, ls] for a in range(count)]
            gr = [gs[a, re, ls] for a in range(count)]
            gi = [gs[a, im, ls] for a in range(count)]
            for b in range(count):
                yr = xr[0] * gr[b] - xi[0] * gi[b]
                yi = xi[0] * gr[b] + xr[0] * gi[b]
                for a in range(1, b + 1):
                    yr = yr + xr[a] * gr[b - a] - xi[a] * gi[b - a]
                    yi = yi + xi[a] * gr[b - a] + xr[a] * gi[b - a]
                ys[b, re, ls] = yr
                ys[b, im, ls] = yi
        return carry

    lax.fori_loop(0, BLOCK // 8, mix, 0)
    for s in range(n):
        for t in range(per):
            spectra = ys[lax.rem(me + s, n) * per + t].astype(jnp.bfloat16)
            conv = jnp.dot(inv_ref[...], spectra, preferred_element_type=jnp.float32)
            held = x_refs[(n - s) % n * per + t][...].astype(jnp.float32)
            out_refs[s * per + t][...] = (conv + skip_ref[...] * held).astype(jnp.bfloat16)


def project_kernel(mats, ops, mode, *refs):
    refs = refs[1:]
    pieces, weights = refs[:ops], refs[ops : ops + ops * mats]
    outs = refs[ops + ops * mats :]
    sums = []
    for m in range(mats):
        total = outs[m][0] if mode != "near" else None
        for p in range(ops):
            term = jnp.dot(pieces[p][...], weights[m * ops + p][0], preferred_element_type=jnp.float32)
            total = term if total is None else total + term
        sums.append(total)
    if mode == "near":
        for m in range(mats):
            outs[m][0] = sums[m]

        @pl.when(pl.program_id(0) == 0)
        def _():
            outs[mats][...] = pieces[0][BLOCK:]
    elif mode == "mix":
        outs[mats][0] = (sums[0] * sums[1]).astype(jnp.bfloat16)
    else:
        outs[mats][0] = sums[0].astype(jnp.bfloat16)


def project(mode, where, pieces, distances, weight, mats, near, t, n):
    rows, width = pieces[0].shape
    channels = weight.shape[2]
    cc = channels // n

    def weight_spec(mat, far):
        return pl.BlockSpec((1, width, cc), lambda s, at: (mat, at[1] ^ far, lax.rem(at[0] + s, n)))

    specs = [pl.BlockSpec((rows, width), lambda s, at: (0, 0))] * len(pieces)
    specs += [weight_spec(mat, far) for mat in mats for far in distances]
    specs += [pl.BlockSpec((1, rows, cc), lambda s, at: (s, t, 0))] * len(near)
    out_spec = pl.BlockSpec((1, rows, cc), lambda s, at: (s, 0, 0))
    if mode == "near":
        shapes = [jax.ShapeDtypeStruct((n, rows, cc), jnp.float32)] * len(mats)
        later = jax.ShapeDtypeStruct((rows - BLOCK, width), jnp.bfloat16)
    else:
        shapes = [jax.ShapeDtypeStruct((n, rows, cc), jnp.bfloat16)]
        later = None
    out_specs = [out_spec] * len(shapes)
    if later is not None:
        shapes.append(later)
        out_specs.append(pl.BlockSpec(later.shape, lambda s, at: (0, 0)))
    flops = 2 * rows * width * channels * len(pieces) * len(mats)
    return pl.pallas_call(
        functools.partial(project_kernel, len(mats), len(pieces), mode),
        out_shape=shapes,
        grid_spec=pltpu.PrefetchScalarGridSpec(
            num_scalar_prefetch=1, grid=(n,), in_specs=specs, out_specs=out_specs
        ),
        compiler_params=pltpu.CompilerParams(vmem_limit_bytes=36 * 1024 * 1024),
        cost_estimate=pl.CostEstimate(flops=flops, bytes_accessed=flops // rows, transcendentals=0),
    )(where, *pieces, *([weight] * (len(mats) * len(distances))), *near)


def convolve(n, per, x, taps, skip):
    cc = taps.shape[1]
    forward, inverse = tables(BLOCK)
    count = n * per
    spectra = pltpu.VMEM((count, 2 * BLOCK, cc), jnp.float32)
    vmem = pl.BlockSpec(memory_space=pltpu.VMEM)
    return pl.pallas_call(
        functools.partial(conv_kernel, n, per),
        out_shape=[jax.ShapeDtypeStruct((BLOCK, cc), jnp.bfloat16)] * count,
        in_specs=[vmem] * (count + 4),
        out_specs=[vmem] * count,
        scratch_shapes=[spectra, spectra, spectra],
        compiler_params=pltpu.CompilerParams(vmem_limit_bytes=40 * 1024 * 1024),
        cost_estimate=pl.CostEstimate(flops=6_000_000_000, bytes_accessed=4_000_000, transcendentals=0),
    )(*x, taps, skip, forward, inverse)


def shift(x, axis, n, by):
    return lax.ppermute(x, axis, [(i, (i + by) % n) for i in range(n)])


def flip(x, n, bit):
    return lax.ppermute(x, "chan", [(i, i ^ bit) for i in range(n)])


def after(x, *others):
    return lax.optimization_barrier((x, *others))[0]


def exchange(parts, n):
    return [parts[0]] + [shift(parts[s], "ctx", n, s) for s in range(1, n)]


def shards(features, filter_taps, skip_gain, in_weight, out_weight):
    f32 = jnp.float32
    n_ctx, n_chan = lax.axis_size("ctx"), lax.axis_size("chan")
    ctx, chan = lax.axis_index("ctx"), lax.axis_index("chan")
    rows, channels = features.shape[0], in_weight.shape[2]
    cc = channels // n_ctx
    per = rows // BLOCK
    paired = n_chan == 4
    taps = lax.dynamic_slice_in_dim(filter_taps, ctx * cc, cc, 1)
    skip = lax.dynamic_slice_in_dim(skip_gain, ctx * cc, cc, 0)[None, :]
    parts = range(per)

    def chunk(x, t):
        return x[t * BLOCK : (t + 1) * BLOCK]

    got, query = [], []
    if paired and cc % 128 == 0:
        where = jnp.stack([ctx, chan]).astype(jnp.int32)
        weight = jnp.transpose(in_weight, (1, 0, 2))
        first = flip(chunk(features, 0), n_chan, 2)
        beside = flip(features, n_chan, 1)
        *near, later = project("near", where, [features, beside], (0, 1), weight, (1, 2, 0), [], 0, n_ctx)
        across, beyond = [first], [flip(first, n_chan, 1)]
        for t in parts[1:]:
            across.append(flip(after(chunk(later, t - 1), beyond[-1]), n_chan, 2))
            beyond.append(flip(across[-1], n_chan, 1))
        far = [[across[t], beyond[t]] for t in parts]
        for t in parts:
            mixed = project("mix", where, far[t], (2, 3), weight, (1, 2), near[:2], t, n_ctx)[0]
            got.append(exchange([mixed[s] for s in range(n_ctx)], n_ctx))
        held = got[-1][0]
        for t in parts:
            pieces = lax.optimization_barrier((*far[t], held))[:2]
            query.append(project("query", where, pieces, (2, 3), weight, (0,), near[2:], t, n_ctx)[0])
    else:
        whole = lax.all_gather(features, "chan", axis=1, tiled=True)
        turned = [jnp.roll(in_weight[:, s], -ctx * cc, axis=1) for s in range(3)]
        for t in parts:
            q, k, v = [jnp.dot(chunk(whole, t), w, preferred_element_type=f32) for w in turned]
            mixed = (k * v).astype(jnp.bfloat16)
            got.append(exchange([mixed[:, s * cc : (s + 1) * cc] for s in range(n_ctx)], n_ctx))
            q = q.astype(jnp.bfloat16)
            query.append(jnp.stack([q[:, s * cc : (s + 1) * cc] for s in range(n_ctx)]))
    x = [got[t][s] for s in range(n_ctx) for t in parts]
    x = lax.optimization_barrier((*x, *query))[: len(x)]
    y = convolve(n_ctx, per, x, taps, skip)

    outs, last = [], None
    for t in parts:
        sends = [y[s * per + t] for s in range(n_ctx)]
        if last is not None:
            sends = lax.optimization_barrier((*sends, *last))[:n_ctx]
        back = last = exchange(sends, n_ctx)
        gated = jnp.zeros((BLOCK, channels), jnp.bfloat16)
        for s in range(n_ctx):
            piece = query[t][(n_ctx - s) % n_ctx].astype(f32) * back[s].astype(f32)
            start = ((ctx - s + n_ctx) % n_ctx) * cc
            gated = lax.dynamic_update_slice(gated, piece.astype(jnp.bfloat16), (0, start))
        if paired:
            far_side = flip(gated, n_chan, 2)
            pieces = [(chan, gated), (chan ^ 1, flip(gated, n_chan, 1))]
            pieces += [(chan ^ 2, far_side), (chan ^ 3, flip(far_side, n_chan, 1))]
        else:
            pieces = [(0, lax.all_gather(gated, "chan", axis=1, tiled=True))]
        total = None
        for owner, piece in pieces:
            depth = piece.shape[1]
            weight = lax.dynamic_slice_in_dim(out_weight, owner * depth, depth, 0)
            term = jnp.dot(piece, weight, preferred_element_type=f32)
            total = term if total is None else total + term
        outs.append(total.astype(jnp.bfloat16))
    return jnp.concatenate(outs, axis=0)


def solution(mesh):
    return jax.shard_map(
        shards,
        mesh=mesh,
        in_specs=(
            P(("grp", "ctx"), "chan"),
            P(None, "chan"),
            P("chan"),
            P(None, None, "chan"),
            P(None, "chan"),
        ),
        out_specs=P(("grp", "ctx"), "chan"),
        check_vma=False,
    )
```
